512 devices in a mesh: win: 16 (over z_lo, core), lat: 32 (over x, z_hi, y).
Axes of the slice: x: 4, y: 4, z: 16 (z_hi: 2, z_lo: 8; z = z_hi * 8 + z_lo), core: 2. Of those that a mesh axis runs over, the one named last changes fastest.
Arguments:
- perturbation: float32 [16, 256, 20, 768], P('win', 'lat'), may hold values from -6 to 6
- lat_offset: int32 [16, 256, 20, 768], P('win', 'lat'), may hold values from -1 to 0
- lon_offset: int32 [16, 256, 20, 768], P('win', 'lat'), may hold values from -4 to 3
- lat_weight: float32 [16, 256, 20, 768], P('win', 'lat'), may hold values from 0 to 0.3
- lon_weight: float32 [16, 256, 20, 768], P('win', 'lat'), may hold values from 0 to 0.3
- spectral_var: float32 [256, 768], P(None, 'lat'), may hold values from 0.5 to 4
Outputs:
- weighted_error: float32 [16, 256, 20, 768], P('win', 'lat')
The draws below stay inside these ranges and needn't reach their ends.
All inputs are finite; a program needn't handle non-finite values.
Results may differ from the reference program's by a relative error of at most 0.0003.
Values sent between devices are 32-bit elements; how exact they have to be, the bound alone decides.
A program may use at most 64 MiB of HBM per device.

```python
import math
import jax
import jax.numpy as jnp
from jax import lax

NLON = 768
LEVELS = 20
STEPS = 4
LON_REACH = 4
NLAT = 256
MM = 384
NWIN = 16


def touch_ends(array, rng, smallest, top_value):
    longest = array.shape.index(max(array.shape))
    spots = []
    for shift in (0, 1):
        where = [jax.random.randint(jax.random.fold_in(rng, axis), (), 0, length) for axis, length in enumerate(array.shape)]
        where[longest] = (where[longest] + shift) % array.shape[longest]
        spots.append(tuple(where))
    return array.at[spots[0]].set(smallest).at[spots[1]].set(top_value)


def steps_of(rng, dims, split, smallest, largest):
    factor_of, own = 1.0, jax.random.fold_in(rng, 6)
    for axis_at, blocks in split:
        steps = jnp.exp(jax.random.uniform(jax.random.fold_in(own, axis_at), (blocks,), jnp.float32, smallest / len(split), largest / len(split)))
        factor_of = factor_of * jnp.repeat(steps, dims[axis_at] // blocks).reshape([-1 if axis == axis_at else 1 for axis in range(len(dims))])
    return factor_of


def scatter_about(own_key, dims, spread, bound, split=(), kind=jnp.bfloat16):
    factor_of = steps_of(own_key, dims, split, -0.22, 0.18) if split else 1.0
    values = jax.random.normal(own_key, dims, jnp.float32) * spread * factor_of
    return jnp.minimum(jnp.maximum(values, -bound), bound).astype(kind)


def setup_inputs(seed: int = 0) -> dict:
    splits = jax.random.split(jax.random.key(seed), 7)
    return {
        "perturbation": scatter_about(splits[0], (NWIN, NLAT, LEVELS, NLON), 1.0, 6.0, ((0, 16), (1, 32)), jnp.float32),
        "lat_offset": touch_ends(jax.random.randint(splits[1], (NWIN, NLAT, LEVELS, NLON), -1, 1), jax.random.fold_in(splits[1], 1), -1, 0).astype(jnp.int32),
        "lon_offset": touch_ends(jax.random.randint(splits[2], (NWIN, NLAT, LEVELS, NLON), -LON_REACH, LON_REACH), jax.random.fold_in(splits[2], 1), -LON_REACH, LON_REACH - 1).astype(jnp.int32),
        "lat_weight": jnp.clip(0.3 * jax.random.uniform(splits[3], (NWIN, NLAT, LEVELS, NLON), jnp.float32) ** steps_of(splits[3], (NWIN, NLAT, LEVELS, NLON), ((0, 16), (1, 32)), -0.2, 0.2), 0.0, 0.3),
        "lon_weight": jnp.clip(0.3 * jax.random.uniform(splits[4], (NWIN, NLAT, LEVELS, NLON), jnp.float32) ** steps_of(splits[4], (NWIN, NLAT, LEVELS, NLON), ((0, 16), (1, 32)), -0.2, 0.2), 0.0, 0.3),
        "spectral_var": jnp.clip(jnp.exp(math.log(4.0) - 2.0794415 * jax.random.uniform(splits[5], (NLAT, 2 * MM), jnp.float32) ** steps_of(splits[5], (NLAT, 2 * MM), ((1, 32),), -0.2, 0.2)), 0.5, 4.0),
    }


def interpolate(padded, lat_offset, lon_offset, lat_weight, lon_weight):
    row_count, level_count, lon_count = lat_offset.shape
    flattened = padded.reshape(-1)
    row_index = jnp.arange(row_count, dtype=jnp.int32)[:, None, None] + 1 + lat_offset
    level_index = jnp.arange(level_count, dtype=jnp.int32)[None, :, None]
    column = jnp.arange(lon_count, dtype=jnp.int32)[None, None, :] + lon_offset
    west_index = column % lon_count
    east_index = (column + 1) % lon_count
    lower_base = (row_index * level_count + level_index) * lon_count
    upper_base = lower_base + level_count * lon_count
    lower_west = jnp.take(flattened, lower_base + west_index)
    lower_east = jnp.take(flattened, lower_base + east_index)
    upper_west = jnp.take(flattened, upper_base + west_index)
    upper_east = jnp.take(flattened, upper_base + east_index)
    mixed_lower = (1.0 - lon_weight) * lower_west + lon_weight * lower_east
    mixed_upper = (1.0 - lon_weight) * upper_west + lon_weight * upper_east
    return (1.0 - lat_weight) * mixed_lower + lat_weight * mixed_upper

def lat_table(lat_count):
    orders = jnp.arange(lat_count, dtype=jnp.int32)[:, None]
    points = jnp.arange(lat_count, dtype=jnp.int32)[None, :]
    angles = ((2 * points + 1) * orders % (4 * lat_count)).astype(jnp.float32) * (math.pi / (2 * lat_count))
    scaling = jnp.where(orders == 0, math.sqrt(1.0 / lat_count), math.sqrt(2.0 / lat_count)).astype(jnp.float32)
    return scaling * jnp.cos(angles)

def propagate(window_args):
    initial, lat_offset, lon_offset, lat_weight, lon_weight = window_args
    current = initial
    for _ in range(STEPS):
        padded = jnp.pad(current, ((1, 1), (0, 0), (0, 0)))
        current = interpolate(padded, lat_offset, lon_offset, lat_weight, lon_weight)
    return current

def reference(perturbation, lat_offset, lon_offset, lat_weight, lon_weight, spectral_var):
    carried = lax.map(propagate, (perturbation, lat_offset, lon_offset, lat_weight, lon_weight))
    previous = jnp.concatenate([jnp.zeros_like(carried[:1]), carried[:-1]], axis=0)
    model_error = perturbation - previous
    half_count = NLON // 2
    lat_basis = lat_table(NLAT)

    def covariance(residue):
        spectrum = jnp.fft.rfft(residue, axis=-1)[..., :half_count]
        coeffs = jnp.concatenate([jnp.real(spectrum), -jnp.imag(spectrum)], axis=-1)
        mode_values = jnp.einsum('py,ylc->plc', lat_basis, coeffs, precision=lax.Precision.HIGHEST)
        scaled = mode_values * spectral_var[:, None, :]
        grid_coeffs = jnp.einsum('py,plc->ylc', lat_basis, scaled, precision=lax.Precision.HIGHEST)
        cosine_part = grid_coeffs[..., :half_count]
        sine_part = grid_coeffs[..., half_count:]
        nyquist = jnp.zeros_like(cosine_part[..., :1])
        complex_part = lax.complex(jnp.concatenate([cosine_part, nyquist], axis=-1), -jnp.concatenate([sine_part, nyquist], axis=-1))
        return jnp.fft.irfft(complex_part, n=NLON, axis=-1)
    return lax.map(covariance, model_error)
```

```python
import math

import jax
import jax.numpy as jnp
import numpy as np
from jax import lax
from jax.experimental import pallas as pl
from jax.experimental.pallas import tpu as pltpu
from jax.sharding import PartitionSpec as P

STEPS = 4
MESH = pl.DeviceIdType.MESH

LEVELS, BAND, NLON, NLAT = 20, 8, 768, 256
CHUNKS = 4
PER = LEVELS // CHUNKS
TILE = 128
TILES = NLON // TILE
HALF_TILES = TILES // 2
UNITS = TILES * PER
HALF_UNITS = UNITS // 2
PEERS = NLAT // BAND
SHARE = NLON // PEERS


def lat_of(half, column):
    return ((column // 4) * 2 + half) * 4 + column % 4


def split_bf16(table):
    high = table.astype(jnp.bfloat16)
    low = (table - high.astype(np.float64)).astype(jnp.bfloat16)
    return high, low


def column_order():
    order = []
    for half in range(2):
        for tile in range(HALF_TILES):
            for column in range(5 * tile, 5 * tile + 5):
                order += [lat_of(half, column) * SHARE + i for i in range(SHARE)]
            order += [lat_of(half, 15) * SHARE + 8 * tile + i for i in range(8)]
    return np.array(order)


def tables():
    half_count = NLON // 2
    points = np.arange(NLON)[:, None]
    orders = np.arange(half_count)[None, :]
    angles = (points * orders % NLON) * (2.0 * math.pi / NLON)
    forward = np.concatenate([np.cos(angles), np.sin(angles)], axis=1)
    weights = np.where(orders == 0, 1.0, 2.0) / NLON
    backward = (forward * np.concatenate([weights, weights], axis=1)).T
    order = column_order()
    modes = np.arange(NLAT)[:, None]
    lats = np.arange(NLAT)[None, :]
    angles = ((2 * lats + 1) * modes % (4 * NLAT)) * (math.pi / (2 * NLAT))
    scaling = np.where(modes == 0, math.sqrt(1.0 / NLAT), math.sqrt(2.0 / NLAT))
    basis = scaling * np.cos(angles)
    return (
        *split_bf16(forward[:, order]),
        *split_bf16(backward[order, :]),
        *split_bf16(basis),
        *split_bf16(np.ascontiguousarray(basis.T)),
    )


def dot(a, b):
    return lax.dot_general(a, b, (((1,), (0,)), ((), ())), preferred_element_type=jnp.float32)


def rows_times_table(rows, high, low):
    count = rows.shape[0]
    rows_high = rows.astype(jnp.bfloat16).astype(jnp.float32)
    both = jnp.concatenate([rows_high, rows - rows_high], axis=0).astype(jnp.bfloat16)
    wide = dot(both, high)
    return wide[:count] + wide[count:] + dot(rows_high.astype(jnp.bfloat16), low)


def table_times_columns(high, low, columns):
    count = columns.shape[1]
    columns_high = columns.astype(jnp.bfloat16).astype(jnp.float32)
    both = jnp.concatenate([columns_high, columns - columns_high], axis=1).astype(jnp.bfloat16)
    wide = dot(high, both)
    return wide[:, :count] + wide[:, count:] + dot(low, columns_high.astype(jnp.bfloat16))


def kernel(
    pert, lat_off, lon_off, lat_w, lon_w, var,
    fwd_high, fwd_low, bwd_high, bwd_low, basis_high, basis_low, basis_t_high, basis_t_low,
    out,
    field, from_south, from_north, prev, coeffs, owned, answer, returned, var_rows, var_tile,
    halo_send, halo_recv, shift_send, shift_recv, out_send, out_recv, back_send, back_recv, var_send, var_recv,
):
    win = lax.axis_index("win")
    lat = lax.axis_index("lat")
    windows = lax.axis_size("win")
    half = (lat // 4) % 2
    column = (lat // 8) * 4 + lat % 4
    my_unit = half * HALF_UNITS + column
    owner = column < HALF_UNITS
    has_south = lat > 0
    has_north = lat < PEERS - 1
    has_prior = win > 0
    has_next = win < windows - 1

    barrier = pltpu.get_barrier_semaphore()

    @pl.loop(0, PEERS)
    def _(peer):
        @pl.when(peer != lat)
        def _():
            pl.semaphore_signal(barrier, 1, device_id={"lat": peer}, device_id_type=MESH)

    @pl.when(has_prior)
    def _():
        pl.semaphore_signal(barrier, 1, device_id={"win": win - 1}, device_id_type=MESH)

    @pl.when(has_next)
    def _():
        pl.semaphore_signal(barrier, 1, device_id={"win": win + 1}, device_id_type=MESH)

    @pl.when(jnp.logical_not(has_south))
    def _():
        from_south[...] = jnp.zeros_like(from_south)

    @pl.when(jnp.logical_not(has_north))
    def _():
        from_north[...] = jnp.zeros_like(from_north)

    pl.semaphore_wait(barrier, PEERS - 1 + has_prior.astype(jnp.int32) + has_next.astype(jnp.int32))

    def source(step):
        return pert if step == 0 else field.at[step - 1]

    def to_north(step, chunk):
        levels = pl.ds(chunk * PER, PER)
        return pltpu.make_async_remote_copy(
            source(step).at[levels, pl.ds(BAND - 1, 1)], from_south.at[step, levels, pl.ds(BAND - 1, 1)],
            halo_send.at[0, step, chunk], halo_recv.at[0, step, chunk],
            device_id={"lat": lat + 1}, device_id_type=MESH)

    def to_south(step, chunk):
        levels = pl.ds(chunk * PER, PER)
        return pltpu.make_async_remote_copy(
            source(step).at[levels, pl.ds(0, 1)], from_north.at[step, levels, pl.ds(0, 1)],
            halo_send.at[1, step, chunk], halo_recv.at[1, step, chunk],
            device_id={"lat": lat - 1}, device_id_type=MESH)

    def send_halo(step, chunk):
        @pl.when(has_north)
        def _():
            to_north(step, chunk).start()

        @pl.when(has_south)
        def _():
            to_south(step, chunk).start()

    for chunk in range(CHUNKS):
        send_halo(0, chunk)

    def share_copy(tile, level):
        target = lat_of(half, tile * 5 + level)
        return target, var, var_rows.at[pl.ds(pl.multiple_of((column % 5) * SHARE, 8), SHARE)], var_recv.at[column % 5]

    @pl.when(owner)
    def _():
        for level in range(PER):
            tile = column // 5
            target = lat_of(half, tile * 5 + level)
            landing = var_rows.at[pl.ds(pl.multiple_of((column % 5) * SHARE, 8), SHARE)]

            @pl.when(target != lat)
            def _():
                pltpu.make_async_remote_copy(
                    var, landing, var_send, var_recv.at[column % 5],
                    device_id={"lat": target}, device_id_type=MESH).start()

            @pl.when(target == lat)
            def _():
                pltpu.make_async_copy(var, landing, var_recv.at[column % 5]).start()

    @pl.when(jnp.logical_not(owner))
    def _():
        for tile in range(HALF_TILES):
            for level in range(PER):
                pltpu.make_async_remote_copy(
                    var.at[pl.ds(8 * tile, 8)], var_rows.at[pl.ds(5 * SHARE, 8)], var_send, var_recv.at[5],
                    device_id={"lat": lat_of(half, tile * 5 + level)}, device_id_type=MESH).start()

    rows_at = lax.broadcasted_iota(jnp.int32, (BAND, NLON), 0)
    lane = lax.broadcasted_iota(jnp.int32, (BAND, TILE), 1)

    def advance(step, level):
        here = source(step)[level]
        south = pltpu.roll(
            jnp.where(rows_at == BAND - 1, from_south[step, level, pl.ds(BAND - 1, 1)], here), 1, 0)
        north = pltpu.roll(
            jnp.where(rows_at == 0, from_north[step, level, pl.ds(0, 1)], here), BAND - 1, 0)
        for tile in range(TILES):
            cut = slice(tile * TILE, (tile + 1) * TILE)
            west = lane + lon_off[level, :, cut]
            east = west + 1
            west_in = (west >= 0) & (west < TILE)
            east_in = (east >= 0) & (east < TILE)
            west = west & (TILE - 1)
            east = east & (TILE - 1)
            weight = lon_w[level, :, cut]
            mixed = []
            for rows in (south, here, north):
                middle = rows[:, cut]
                after = (tile + 1) % TILES * TILE
                before = (tile - 1) % TILES * TILE
                beside = jnp.where(
                    lane < TILE // 2, rows[:, after : after + TILE], rows[:, before : before + TILE])
                near = jnp.where(
                    west_in, jnp.take_along_axis(middle, west, 1), jnp.take_along_axis(beside, west, 1))
                far = jnp.where(
                    east_in, jnp.take_along_axis(middle, east, 1), jnp.take_along_axis(beside, east, 1))
                mixed.append((1.0 - weight) * near + weight * far)
            below = lat_off[level, :, cut] < 0
            lower = jnp.where(below, mixed[0], mixed[1])
            upper = jnp.where(below, mixed[1], mixed[2])
            part = lat_w[level, :, cut]
            field[step, level, :, cut] = (1.0 - part) * lower + part * upper

    def shift(chunk):
        levels = pl.ds(chunk * PER, PER)
        return pltpu.make_async_remote_copy(
            field.at[STEPS - 1, levels], prev.at[levels], shift_send.at[chunk], shift_recv.at[chunk],
            device_id={"win": win + 1}, device_id_type=MESH)

    for step in range(STEPS):
        for chunk in range(CHUNKS):
            @pl.when(has_south)
            def _():
                to_north(step, chunk).wait_recv()

            @pl.when(has_north)
            def _():
                to_south(step, chunk).wait_recv()

            @pl.loop(chunk * PER, (chunk + 1) * PER)
            def _(level):
                advance(step, level)

            if step < STEPS - 1:
                send_halo(step + 1, chunk)
            else:
                @pl.when(has_next)
                def _():
                    shift(chunk).start()

    my_rows = pl.ds(pl.multiple_of(lat * BAND, BAND), BAND)

    for chunk in range(CHUNKS):
        levels = pl.ds(chunk * PER, PER)

        @pl.when(has_prior)
        def _():
            shift(chunk).wait_recv()

        @pl.when(jnp.logical_not(has_prior))
        def _():
            prev[levels] = jnp.zeros((PER, BAND, NLON), jnp.float32)

        error = (pert[levels] - prev[levels]).reshape(PER * BAND, NLON)
        result = rows_times_table(error, fwd_high[...], fwd_low[...])
        for tile in range(TILES):
            coeffs[chunk, pl.ds(tile * PER, PER)] = result[:, tile * TILE : (tile + 1) * TILE].reshape(
                PER, BAND, TILE)

        @pl.loop(0, UNITS)
        def _(unit):
            target = lat_of(unit // HALF_UNITS, unit % HALF_UNITS)

            @pl.when(target != lat)
            def _():
                pltpu.make_async_remote_copy(
                    coeffs.at[chunk, unit], owned.at[chunk, my_rows], out_send.at[chunk], out_recv.at[chunk],
                    device_id={"lat": target}, device_id_type=MESH).start()

            @pl.when(target == lat)
            def _():
                pltpu.make_async_copy(
                    coeffs.at[chunk, unit], owned.at[chunk, my_rows], out_recv.at[chunk]).start()

    @pl.when(owner)
    def _():
        for share in range(5):
            piece = var_rows.at[pl.ds(share * SHARE, SHARE)]
            pltpu.make_async_copy(piece, piece, var_recv.at[share]).wait()
        piece = var_rows.at[pl.ds(5 * SHARE, 8)]
        pltpu.make_async_copy(piece, piece, var_recv.at[5]).wait()
        var_tile[...] = var_rows[...].T

        for chunk in range(CHUNKS):
            pltpu.make_async_copy(owned.at[chunk], owned.at[chunk], out_recv.at[chunk]).wait()
            modes = table_times_columns(basis_high[...], basis_low[...], owned[chunk])
            answer[chunk] = table_times_columns(
                basis_t_high[...], basis_t_low[...], modes * var_tile[...])

            @pl.loop(0, PEERS)
            def _(peer):
                rows = pl.ds(pl.multiple_of(peer * BAND, BAND), BAND)

                @pl.when(peer != lat)
                def _():
                    pltpu.make_async_remote_copy(
                        answer.at[chunk, rows], returned.at[chunk, my_unit], back_send.at[chunk],
                        back_recv.at[chunk], device_id={"lat": peer}, device_id_type=MESH).start()

                @pl.when(peer == lat)
                def _():
                    pltpu.make_async_copy(
                        answer.at[chunk, rows], returned.at[chunk, my_unit], back_recv.at[chunk]).start()

    for chunk in range(CHUNKS):
        pltpu.make_async_copy(returned.at[chunk], returned.at[chunk], back_recv.at[chunk]).wait()
        rows = jnp.concatenate(
            [returned[chunk, pl.ds(tile * PER, PER)].reshape(PER * BAND, TILE) for tile in range(TILES)], axis=1)
        result = rows_times_table(rows, bwd_high[...], bwd_low[...])
        out[pl.ds(chunk * PER, PER)] = result.reshape(PER, BAND, NLON)

    for step in range(STEPS):
        for chunk in range(CHUNKS):
            @pl.when(has_north)
            def _():
                to_north(step, chunk).wait_send()

            @pl.when(has_south)
            def _():
                to_south(step, chunk).wait_send()

    for chunk in range(CHUNKS):
        @pl.when(has_next)
        def _():
            shift(chunk).wait_send()

        @pl.when(owner)
        def _():
            part = coeffs.at[chunk, pl.ds(0, UNITS - 1)]
            pltpu.make_async_copy(part, part, out_send.at[chunk]).wait()
            part = answer.at[chunk, pl.ds(0, NLAT - BAND)]
            pltpu.make_async_copy(part, part, back_send.at[chunk]).wait()

        @pl.when(jnp.logical_not(owner))
        def _():
            part = coeffs.at[chunk]
            pltpu.make_async_copy(part, part, out_send.at[chunk]).wait()

    @pl.when(owner)
    def _():
        part = var_rows.at[pl.ds(0, 4 * SHARE)]
        pltpu.make_async_copy(part, part, var_send).wait()

    @pl.when(jnp.logical_not(owner))
    def _():
        part = var_rows.at[pl.ds(0, HALF_TILES * PER * 8)]
        pltpu.make_async_copy(part, part, var_send).wait()


def body(perturbation, lat_offset, lon_offset, lat_weight, lon_weight, spectral_var):
    def levels_first(x):
        return jnp.transpose(x[0], (1, 0, 2))

    grid = (LEVELS, BAND, NLON)
    f32 = jnp.float32
    dma = pltpu.SemaphoreType.DMA
    vmem = pl.BlockSpec(memory_space=pltpu.VMEM)
    constants = [jnp.asarray(table) for table in tables()]
    result = pl.pallas_call(
        kernel,
        out_shape=jax.ShapeDtypeStruct(grid, f32),
        in_specs=[vmem] * (6 + len(constants)),
        out_specs=vmem,
        scratch_shapes=[
            pltpu.VMEM((STEPS, *grid), f32),
            pltpu.VMEM((STEPS, *grid), f32),
            pltpu.VMEM((STEPS, *grid), f32),
            pltpu.VMEM(grid, f32),
            pltpu.VMEM((CHUNKS, UNITS, BAND, TILE), f32),
            pltpu.VMEM((CHUNKS, NLAT, TILE), f32),
            pltpu.VMEM((CHUNKS, NLAT, TILE), f32),
            pltpu.VMEM((CHUNKS, UNITS, BAND, TILE), f32),
            pltpu.VMEM((TILE, NLAT), f32),
            pltpu.VMEM((NLAT, TILE), f32),
            dma((2, STEPS, CHUNKS)),
            dma((2, STEPS, CHUNKS)),
            dma((CHUNKS,)),
            dma((CHUNKS,)),
            dma((CHUNKS,)),
            dma((CHUNKS,)),
            dma((CHUNKS,)),
            dma((CHUNKS,)),
            dma,
            dma((6,)),
        ],
        compiler_params=pltpu.CompilerParams(
            collective_id=0, has_side_effects=True, vmem_limit_bytes=48 * 2**20),
    )(
        *[levels_first(x) for x in (perturbation, lat_offset, lon_offset, lat_weight, lon_weight)],
        spectral_var.T,
        *constants,
    )
    return jnp.transpose(result, (1, 0, 2))[None]


def solution(mesh):
    block = P("win", "lat", None, None)
    return jax.shard_map(
        body, mesh=mesh, in_specs=(block, block, block, block, block, P(None, "lat")), out_specs=block,
        check_vma=False)
```

```python
import math

import jax
import jax.numpy as jnp
import numpy as np
from jax import lax
from jax.experimental import pallas as pl
from jax.experimental.pallas import tpu as pltpu
from jax.sharding import PartitionSpec as P

STEPS = 4
MESH = pl.DeviceIdType.MESH

LEVELS, BAND, NLON, NLAT = 20, 8, 768, 256
CHUNKS = 4
PER = LEVELS // CHUNKS
TILE = 128
TILES = NLON // TILE
HALF_TILES = TILES // 2
UNITS = TILES * PER
HALF_UNITS = UNITS // 2
PEERS = NLAT // BAND
SHARE = NLON // PEERS
FETCHED = 14


def lat_of(half, column):
    return ((column // 4) * 2 + half) * 4 + column % 4


def split_bf16(table):
    high = table.astype(jnp.bfloat16)
    low = (table - high.astype(np.float64)).astype(jnp.bfloat16)
    return high, low


def column_order():
    order = []
    for half in range(2):
        for tile in range(HALF_TILES):
            for column in range(5 * tile, 5 * tile + 5):
                order += [lat_of(half, column) * SHARE + i for i in range(SHARE)]
            order += [lat_of(half, 15) * SHARE + 8 * tile + i for i in range(8)]
    return np.array(order)


def tables():
    half_count = NLON // 2
    points = np.arange(NLON)[:, None]
    orders = np.arange(half_count)[None, :]
    angles = (points * orders % NLON) * (2.0 * math.pi / NLON)
    forward = np.concatenate([np.cos(angles), np.sin(angles)], axis=1)
    weights = np.where(orders == 0, 1.0, 2.0) / NLON
    backward = (forward * np.concatenate([weights, weights], axis=1)).T
    order = column_order()
    modes = np.arange(NLAT)[:, None]
    lats = np.arange(NLAT)[None, :]
    angles = ((2 * lats + 1) * modes % (4 * NLAT)) * (math.pi / (2 * NLAT))
    scaling = np.where(modes == 0, math.sqrt(1.0 / NLAT), math.sqrt(2.0 / NLAT))
    basis = scaling * np.cos(angles)
    return (
        *split_bf16(forward[:, order]),
        *split_bf16(backward[order, :]),
        *split_bf16(basis),
        *split_bf16(np.ascontiguousarray(basis.T)),
    )


def dot(a, b):
    return lax.dot_general(a, b, (((1,), (0,)), ((), ())), preferred_element_type=jnp.float32)


def rows_times_table(rows, high, low):
    count = rows.shape[0]
    rows_high = rows.astype(jnp.bfloat16).astype(jnp.float32)
    both = jnp.concatenate([rows_high, rows - rows_high], axis=0).astype(jnp.bfloat16)
    wide = dot(both, high)
    return wide[:count] + wide[count:] + dot(rows_high.astype(jnp.bfloat16), low)


def table_times_columns(high, low, columns):
    count = columns.shape[1]
    columns_high = columns.astype(jnp.bfloat16).astype(jnp.float32)
    both = jnp.concatenate([columns_high, columns - columns_high], axis=1).astype(jnp.bfloat16)
    wide = dot(high, both)
    return wide[:, :count] + wide[:, count:] + dot(low, columns_high.astype(jnp.bfloat16))


def kernel(
    *refs,
):
    sources, (out, *fetched), rest = refs[:FETCHED], refs[FETCHED : 2 * FETCHED + 1], refs[2 * FETCHED + 1 :]
    (pert, lat_off, lon_off, lat_w, lon_w, var,
     fwd_high, fwd_low, bwd_high, bwd_low, basis_high, basis_low, basis_t_high, basis_t_low) = fetched
    (
        field, from_south, from_north, prev, coeffs, owned, answer, returned, var_rows, var_tile,
        halo_send, halo_recv, shift_send, shift_recv, out_send, out_recv, back_send, back_recv, var_send, var_recv,
        fetch_sem,
    ) = rest
    fetches = [
        pltpu.make_async_copy(source, target, fetch_sem.at[i])
        for i, (source, target) in enumerate(zip(sources, fetched))
    ]
    for fetch in fetches:
        fetch.start()

    win = lax.axis_index("win")
    lat = lax.axis_index("lat")
    windows = lax.axis_size("win")
    half = (lat // 4) % 2
    column = (lat // 8) * 4 + lat % 4
    my_unit = half * HALF_UNITS + column
    owner = column < HALF_UNITS
    has_prior = win > 0
    has_next = win < windows - 1
    has_south = has_next & (lat > 0)
    has_north = has_next & (lat < PEERS - 1)

    barrier = pltpu.get_barrier_semaphore()

    @pl.loop(0, PEERS)
    def _(peer):
        @pl.when(peer != lat)
        def _():
            pl.semaphore_signal(barrier, 1, device_id={"lat": peer}, device_id_type=MESH)

    @pl.when(has_prior)
    def _():
        pl.semaphore_signal(barrier, 1, device_id={"win": win - 1}, device_id_type=MESH)

    @pl.when(has_next)
    def _():
        pl.semaphore_signal(barrier, 1, device_id={"win": win + 1}, device_id_type=MESH)

    @pl.when(jnp.logical_not(has_south))
    def _():
        from_south[...] = jnp.zeros_like(from_south)

    @pl.when(jnp.logical_not(has_north))
    def _():
        from_north[...] = jnp.zeros_like(from_north)

    for fetch in fetches[:6]:
        fetch.wait()
    pl.semaphore_wait(barrier, PEERS - 1 + has_prior.astype(jnp.int32) + has_next.astype(jnp.int32))

    def source(step):
        return pert if step == 0 else field.at[step - 1]

    def to_north(step, chunk):
        levels = pl.ds(chunk * PER, PER)
        return pltpu.make_async_remote_copy(
            source(step).at[levels, pl.ds(BAND - 1, 1)], from_south.at[step, levels, pl.ds(BAND - 1, 1)],
            halo_send.at[0, step, chunk], halo_recv.at[0, step, chunk],
            device_id={"lat": lat + 1}, device_id_type=MESH)

    def to_south(step, chunk):
        levels = pl.ds(chunk * PER, PER)
        return pltpu.make_async_remote_copy(
            source(step).at[levels, pl.ds(0, 1)], from_north.at[step, levels, pl.ds(0, 1)],
            halo_send.at[1, step, chunk], halo_recv.at[1, step, chunk],
            device_id={"lat": lat - 1}, device_id_type=MESH)

    def send_halo(step, chunk):
        @pl.when(has_north)
        def _():
            to_north(step, chunk).start()

        @pl.when(has_south)
        def _():
            to_south(step, chunk).start()

    for chunk in range(CHUNKS):
        send_halo(0, chunk)

    @pl.when(owner)
    def _():
        for level in range(PER):
            tile = column // 5
            target = lat_of(half, tile * 5 + level)
            landing = var_rows.at[pl.ds(pl.multiple_of((column % 5) * SHARE, 8), SHARE)]

            @pl.when(target != lat)
            def _():
                pltpu.make_async_remote_copy(
                    var, landing, var_send, var_recv.at[column % 5],
                    device_id={"lat": target}, device_id_type=MESH).start()

            @pl.when(target == lat)
            def _():
                pltpu.make_async_copy(var, landing, var_recv.at[column % 5]).start()

    @pl.when(jnp.logical_not(owner))
    def _():
        for tile in range(HALF_TILES):
            for level in range(PER):
                pltpu.make_async_remote_copy(
                    var.at[pl.ds(8 * tile, 8)], var_rows.at[pl.ds(5 * SHARE, 8)], var_send, var_recv.at[5],
                    device_id={"lat": lat_of(half, tile * 5 + level)}, device_id_type=MESH).start()

    rows_at = lax.broadcasted_iota(jnp.int32, (BAND, NLON), 0)
    lane = lax.broadcasted_iota(jnp.int32, (BAND, TILE), 1)

    def advance(step, level):
        here = source(step)[level]
        south = pltpu.roll(
            jnp.where(rows_at == BAND - 1, from_south[step, level, pl.ds(BAND - 1, 1)], here), 1, 0)
        north = pltpu.roll(
            jnp.where(rows_at == 0, from_north[step, level, pl.ds(0, 1)], here), BAND - 1, 0)
        for tile in range(TILES):
            cut = slice(tile * TILE, (tile + 1) * TILE)
            west = lane + lon_off[level, :, cut]
            east = west + 1
            west_in = (west >= 0) & (west < TILE)
            east_in = (east >= 0) & (east < TILE)
            west = west & (TILE - 1)
            east = east & (TILE - 1)
            weight = lon_w[level, :, cut]
            mixed = []
            for rows in (south, here, north):
                middle = rows[:, cut]
                after = (tile + 1) % TILES * TILE
                before = (tile - 1) % TILES * TILE
                beside = jnp.where(
                    lane < TILE // 2, rows[:, after : after + TILE], rows[:, before : before + TILE])
                near = jnp.where(
                    west_in, jnp.take_along_axis(middle, west, 1), jnp.take_along_axis(beside, west, 1))
                far = jnp.where(
                    east_in, jnp.take_along_axis(middle, east, 1), jnp.take_along_axis(beside, east, 1))
                mixed.append((1.0 - weight) * near + weight * far)
            below = lat_off[level, :, cut] < 0
            lower = jnp.where(below, mixed[0], mixed[1])
            upper = jnp.where(below, mixed[1], mixed[2])
            part = lat_w[level, :, cut]
            field[step, level, :, cut] = (1.0 - part) * lower + part * upper

    def shift(chunk):
        levels = pl.ds(chunk * PER, PER)
        return pltpu.make_async_remote_copy(
            field.at[STEPS - 1, levels], prev.at[levels], shift_send.at[chunk], shift_recv.at[chunk],
            device_id={"win": win + 1}, device_id_type=MESH)

    for step in range(STEPS):
        for chunk in range(CHUNKS):
            @pl.when(has_south)
            def _():
                to_north(step, chunk).wait_recv()

            @pl.when(has_north)
            def _():
                to_south(step, chunk).wait_recv()

            @pl.when(has_next)
            def _():
                @pl.loop(chunk * PER, (chunk + 1) * PER)
                def _(level):
                    advance(step, level)

            if step < STEPS - 1:
                send_halo(step + 1, chunk)
            else:
                @pl.when(has_next)
                def _():
                    shift(chunk).start()

    for fetch in fetches[6:]:
        fetch.wait()

    my_rows = pl.ds(pl.multiple_of(lat * BAND, BAND), BAND)

    for chunk in range(CHUNKS):
        levels = pl.ds(chunk * PER, PER)

        @pl.when(has_prior)
        def _():
            shift(chunk).wait_recv()

        @pl.when(jnp.logical_not(has_prior))
        def _():
            prev[levels] = jnp.zeros((PER, BAND, NLON), jnp.float32)

        error = (pert[levels] - prev[levels]).reshape(PER * BAND, NLON)
        result = rows_times_table(error, fwd_high[...], fwd_low[...])
        for tile in range(TILES):
            coeffs[chunk, pl.ds(tile * PER, PER)] = result[:, tile * TILE : (tile + 1) * TILE].reshape(
                PER, BAND, TILE)

        @pl.loop(0, UNITS)
        def _(unit):
            target = lat_of(unit // HALF_UNITS, unit % HALF_UNITS)

            @pl.when(target != lat)
            def _():
                pltpu.make_async_remote_copy(
                    coeffs.at[chunk, unit], owned.at[chunk, my_rows], out_send.at[chunk], out_recv.at[chunk],
                    device_id={"lat": target}, device_id_type=MESH).start()

            @pl.when(target == lat)
            def _():
                pltpu.make_async_copy(
                    coeffs.at[chunk, unit], owned.at[chunk, my_rows], out_recv.at[chunk]).start()

    @pl.when(owner)
    def _():
        for share in range(5):
            piece = var_rows.at[pl.ds(share * SHARE, SHARE)]
            pltpu.make_async_copy(piece, piece, var_recv.at[share]).wait()
        piece = var_rows.at[pl.ds(5 * SHARE, 8)]
        pltpu.make_async_copy(piece, piece, var_recv.at[5]).wait()
        var_tile[...] = var_rows[...].T

        for chunk in range(CHUNKS):
            pltpu.make_async_copy(owned.at[chunk], owned.at[chunk], out_recv.at[chunk]).wait()
            modes = table_times_columns(basis_high[...], basis_low[...], owned[chunk])
            answer[chunk] = table_times_columns(
                basis_t_high[...], basis_t_low[...], modes * var_tile[...])

            @pl.loop(0, PEERS)
            def _(peer):
                rows = pl.ds(pl.multiple_of(peer * BAND, BAND), BAND)

                @pl.when(peer != lat)
                def _():
                    pltpu.make_async_remote_copy(
                        answer.at[chunk, rows], returned.at[chunk, my_unit], back_send.at[chunk],
                        back_recv.at[chunk], device_id={"lat": peer}, device_id_type=MESH).start()

                @pl.when(peer == lat)
                def _():
                    pltpu.make_async_copy(
                        answer.at[chunk, rows], returned.at[chunk, my_unit], back_recv.at[chunk]).start()

    for chunk in range(CHUNKS):
        pltpu.make_async_copy(returned.at[chunk], returned.at[chunk], back_recv.at[chunk]).wait()
        rows = jnp.concatenate(
            [returned[chunk, pl.ds(tile * PER, PER)].reshape(PER * BAND, TILE) for tile in range(TILES)], axis=1)
        result = rows_times_table(rows, bwd_high[...], bwd_low[...])
        out[pl.ds(chunk * PER, PER)] = result.reshape(PER, BAND, NLON)

    for step in range(STEPS):
        for chunk in range(CHUNKS):
            @pl.when(has_north)
            def _():
                to_north(step, chunk).wait_send()

            @pl.when(has_south)
            def _():
                to_south(step, chunk).wait_send()

    for chunk in range(CHUNKS):
        @pl.when(has_next)
        def _():
            shift(chunk).wait_send()

        @pl.when(owner)
        def _():
            part = coeffs.at[chunk, pl.ds(0, UNITS - 1)]
            pltpu.make_async_copy(part, part, out_send.at[chunk]).wait()
            part = answer.at[chunk, pl.ds(0, NLAT - BAND)]
            pltpu.make_async_copy(part, part, back_send.at[chunk]).wait()

        @pl.when(jnp.logical_not(owner))
        def _():
            part = coeffs.at[chunk]
            pltpu.make_async_copy(part, part, out_send.at[chunk]).wait()

    @pl.when(owner)
    def _():
        part = var_rows.at[pl.ds(0, 4 * SHARE)]
        pltpu.make_async_copy(part, part, var_send).wait()

    @pl.when(jnp.logical_not(owner))
    def _():
        part = var_rows.at[pl.ds(0, HALF_TILES * PER * 8)]
        pltpu.make_async_copy(part, part, var_send).wait()


def body(perturbation, lat_offset, lon_offset, lat_weight, lon_weight, spectral_var):
    def levels_first(x):
        return jnp.transpose(x[0], (1, 0, 2))

    grid = (LEVELS, BAND, NLON)
    f32 = jnp.float32
    dma = pltpu.SemaphoreType.DMA
    operands = [
        *[levels_first(x) for x in (perturbation, lat_offset, lon_offset, lat_weight, lon_weight)],
        spectral_var.T,
        *[jnp.asarray(table) for table in tables()],
    ]
    result = pl.pallas_call(
        kernel,
        out_shape=jax.ShapeDtypeStruct(grid, f32),
        in_specs=[pl.BlockSpec(memory_space=pl.ANY)] * FETCHED,
        out_specs=pl.BlockSpec(memory_space=pltpu.VMEM),
        scratch_shapes=[
            *[pltpu.VMEM(x.shape, x.dtype) for x in operands],
            pltpu.VMEM((STEPS, *grid), f32),
            pltpu.VMEM((STEPS, *grid), f32),
            pltpu.VMEM((STEPS, *grid), f32),
            pltpu.VMEM(grid, f32),
            pltpu.VMEM((CHUNKS, UNITS, BAND, TILE), f32),
            pltpu.VMEM((CHUNKS, NLAT, TILE), f32),
            pltpu.VMEM((CHUNKS, NLAT, TILE), f32),
            pltpu.VMEM((CHUNKS, UNITS, BAND, TILE), f32),
            pltpu.VMEM((TILE, NLAT), f32),
            pltpu.VMEM((NLAT, TILE), f32),
            dma((2, STEPS, CHUNKS)),
            dma((2, STEPS, CHUNKS)),
            dma((CHUNKS,)),
            dma((CHUNKS,)),
            dma((CHUNKS,)),
            dma((CHUNKS,)),
            dma((CHUNKS,)),
            dma((CHUNKS,)),
            dma,
            dma((6,)),
            dma((FETCHED,)),
        ],
        compiler_params=pltpu.CompilerParams(
            collective_id=0, has_side_effects=True, vmem_limit_bytes=60 * 2**20),
    )(*operands)
    return jnp.transpose(result, (1, 0, 2))[None]


def solution(mesh):
    block = P("win", "lat", None, None)
    return jax.shard_map(
        body, mesh=mesh, in_specs=(block, block, block, block, block, P(None, "lat")), out_specs=block,
        check_vma=False)
```

```python
import math

import jax
import jax.numpy as jnp
import numpy as np
from jax import lax
from jax.experimental import pallas as pl
from jax.experimental.pallas import tpu as pltpu
from jax.sharding import PartitionSpec as P

STEPS = 4
MESH = pl.DeviceIdType.MESH

LEVELS, BAND, NLON, NLAT = 20, 8, 768, 256
CHUNKS = 5
PER = LEVELS // CHUNKS
TILE = 128
TILES = NLON // TILE
HALF_TILES = TILES // 2
UNITS = TILES * PER
HALF_UNITS = UNITS // 2
PEERS = NLAT // BAND
SHARE = NLON // PEERS
FETCHED = 14


def lat_of(half, column):
    inner = column < 8
    x = inner * (column // 2) + (1 - inner) * (column % 4)
    y = inner * (1 + column % 2) + (1 - inner) * (column // 12) * 3
    return (x * 2 + half) * 4 + y


def owner_of(half, place, chunk):
    return lat_of(half, place + 4 * (chunk % 2) * (place // 8))


def split_bf16(table):
    high = table.astype(jnp.bfloat16)
    low = (table - high.astype(np.float64)).astype(jnp.bfloat16)
    return high, low


def column_order():
    order = []
    for half in range(2):
        for tile in range(HALF_TILES):
            for column in range(5 * tile, 5 * tile + 5):
                order += [lat_of(half, column) * SHARE + i for i in range(SHARE)]
            order += [lat_of(half, 15) * SHARE + 8 * tile + i for i in range(8)]
    return np.array(order)


def tables():
    half_count = NLON // 2
    points = np.arange(NLON)[:, None]
    orders = np.arange(half_count)[None, :]
    angles = (points * orders % NLON) * (2.0 * math.pi / NLON)
    forward = np.concatenate([np.cos(angles), np.sin(angles)], axis=1)
    weights = np.where(orders == 0, 1.0, 2.0) / NLON
    backward = (forward * np.concatenate([weights, weights], axis=1)).T
    order = column_order()
    modes = np.arange(NLAT)[:, None]
    lats = np.arange(NLAT)[None, :]
    angles = ((2 * lats + 1) * modes % (4 * NLAT)) * (math.pi / (2 * NLAT))
    scaling = np.where(modes == 0, math.sqrt(1.0 / NLAT), math.sqrt(2.0 / NLAT))
    basis = scaling * np.cos(angles)
    return (
        *split_bf16(forward[:, order]),
        *split_bf16(backward[order, :]),
        *split_bf16(basis),
        *split_bf16(np.ascontiguousarray(basis.T)),
    )


def dot(a, b):
    return lax.dot_general(a, b, (((1,), (0,)), ((), ())), preferred_element_type=jnp.float32)


def rows_times_table(rows, high, low):
    count = rows.shape[0]
    rows_high = rows.astype(jnp.bfloat16).astype(jnp.float32)
    both = jnp.concatenate([rows_high, rows - rows_high], axis=0).astype(jnp.bfloat16)
    wide = dot(both, high)
    return wide[:count] + wide[count:] + dot(rows_high.astype(jnp.bfloat16), low)


def table_times_columns(high, low, columns):
    count = columns.shape[1]
    columns_high = columns.astype(jnp.bfloat16).astype(jnp.float32)
    both = jnp.concatenate([columns_high, columns - columns_high], axis=1).astype(jnp.bfloat16)
    wide = dot(high, both)
    return wide[:, :count] + wide[:, count:] + dot(low, columns_high.astype(jnp.bfloat16))


def kernel(
    *refs,
):
    sources, (out, *fetched), rest = refs[:FETCHED], refs[FETCHED : 2 * FETCHED + 1], refs[2 * FETCHED + 1 :]
    (pert, lat_off, lon_off, lat_w, lon_w, var,
     fwd_high, fwd_low, bwd_high, bwd_low, basis_high, basis_low, basis_t_high, basis_t_low) = fetched
    (
        field, from_south, from_north, prev, coeffs, owned, answer, returned, var_rows, var_tile,
        halo_send, halo_recv, shift_send, shift_recv, out_send, out_recv, back_send, back_recv, var_send, var_recv,
        fetch_sem,
    ) = rest
    fetches = [
        pltpu.make_async_copy(source, target, fetch_sem.at[i])
        for i, (source, target) in enumerate(zip(sources, fetched))
    ]
    for fetch in fetches:
        fetch.start()

    win = lax.axis_index("win")
    lat = lax.axis_index("lat")
    windows = lax.axis_size("win")
    half = (lat // 4) % 2
    x, y = lat // 8, lat % 4
    column = jnp.where(y == 0, 8 + x, jnp.where(y == 3, 12 + x, 2 * x + y - 1))
    inner = column < 8
    my_unit = half * HALF_UNITS + jnp.where(inner, column, 8 + x)

    def owns(chunk):
        return inner | (y == 0 if chunk % 2 == 0 else y == 3)

    has_prior = win > 0
    has_next = win < windows - 1
    has_south = has_next & (lat > 0)
    has_north = has_next & (lat < PEERS - 1)

    barrier = pltpu.get_barrier_semaphore()

    @pl.loop(0, PEERS)
    def _(peer):
        @pl.when(peer != lat)
        def _():
            pl.semaphore_signal(barrier, 1, device_id={"lat": peer}, device_id_type=MESH)

    @pl.when(has_prior)
    def _():
        pl.semaphore_signal(barrier, 1, device_id={"win": win - 1}, device_id_type=MESH)

    @pl.when(has_next)
    def _():
        pl.semaphore_signal(barrier, 1, device_id={"win": win + 1}, device_id_type=MESH)

    @pl.when(jnp.logical_not(has_south))
    def _():
        from_south[...] = jnp.zeros_like(from_south)

    @pl.when(jnp.logical_not(has_north))
    def _():
        from_north[...] = jnp.zeros_like(from_north)

    for fetch in fetches[:6]:
        fetch.wait()
    pl.semaphore_wait(barrier, PEERS - 1 + has_prior.astype(jnp.int32) + has_next.astype(jnp.int32))

    def source(step):
        return pert if step == 0 else field.at[step - 1]

    def to_north(step, chunk):
        levels = pl.ds(chunk * PER, PER)
        return pltpu.make_async_remote_copy(
            source(step).at[levels, pl.ds(BAND - 1, 1)], from_south.at[step, levels, pl.ds(BAND - 1, 1)],
            halo_send.at[0, step, chunk], halo_recv.at[0, step, chunk],
            device_id={"lat": lat + 1}, device_id_type=MESH)

    def to_south(step, chunk):
        levels = pl.ds(chunk * PER, PER)
        return pltpu.make_async_remote_copy(
            source(step).at[levels, pl.ds(0, 1)], from_north.at[step, levels, pl.ds(0, 1)],
            halo_send.at[1, step, chunk], halo_recv.at[1, step, chunk],
            device_id={"lat": lat - 1}, device_id_type=MESH)

    def send_halo(step, chunk):
        @pl.when(has_north)
        def _():
            to_north(step, chunk).start()

        @pl.when(has_south)
        def _():
            to_south(step, chunk).start()

    for chunk in range(CHUNKS):
        send_halo(0, chunk)

    whole = column < 15
    share_tile = column // 5
    share_first = share_tile * PER
    share_count = jnp.where(share_tile == 2, 2 * PER, PER)
    landing = var_rows.at[pl.ds(pl.multiple_of((column % 5) * SHARE, 8), SHARE)]
    rest_landing = var_rows.at[pl.ds(5 * SHARE, 8)]

    def share_to(target, i):
        return pltpu.make_async_remote_copy(
            var, landing, var_send.at[i], var_recv.at[column % 5], device_id={"lat": target}, device_id_type=MESH)

    def rest_to(target, i):
        tile = jnp.minimum(i // PER, 2)
        return pltpu.make_async_remote_copy(
            var.at[pl.ds(pl.multiple_of(8 * tile, 8), 8)], rest_landing, var_send.at[i], var_recv.at[5],
            device_id={"lat": target}, device_id_type=MESH)

    @pl.when(whole)
    def _():
        @pl.loop(0, share_count)
        def _(i):
            target = lat_of(half, share_first + i)

            @pl.when(target != lat)
            def _():
                share_to(target, i).start()

            @pl.when(target == lat)
            def _():
                pltpu.make_async_copy(var, landing, var_recv.at[column % 5]).start()

    @pl.when(jnp.logical_not(whole))
    def _():
        @pl.loop(0, 15)
        def _(i):
            rest_to(lat_of(half, i), i).start()

        pltpu.make_async_copy(var.at[pl.ds(16, 8)], rest_landing, var_recv.at[5]).start()

    rows_at = lax.broadcasted_iota(jnp.int32, (BAND, NLON), 0)
    lane = lax.broadcasted_iota(jnp.int32, (BAND, TILE), 1)

    def advance(step, level):
        here = source(step)[level]
        south = pltpu.roll(
            jnp.where(rows_at == BAND - 1, from_south[step, level, pl.ds(BAND - 1, 1)], here), 1, 0)
        north = pltpu.roll(
            jnp.where(rows_at == 0, from_north[step, level, pl.ds(0, 1)], here), BAND - 1, 0)
        for tile in range(TILES):
            cut = slice(tile * TILE, (tile + 1) * TILE)
            west = lane + lon_off[level, :, cut]
            east = west + 1
            west_in = (west >= 0) & (west < TILE)
            east_in = (east >= 0) & (east < TILE)
            west = west & (TILE - 1)
            east = east & (TILE - 1)
            weight = lon_w[level, :, cut]
            mixed = []
            for rows in (south, here, north):
                middle = rows[:, cut]
                after = (tile + 1) % TILES * TILE
                before = (tile - 1) % TILES * TILE
                beside = jnp.where(
                    lane < TILE // 2, rows[:, after : after + TILE], rows[:, before : before + TILE])
                near = jnp.where(
                    west_in, jnp.take_along_axis(middle, west, 1), jnp.take_along_axis(beside, west, 1))
                far = jnp.where(
                    east_in, jnp.take_along_axis(middle, east, 1), jnp.take_along_axis(beside, east, 1))
                mixed.append((1.0 - weight) * near + weight * far)
            below = lat_off[level, :, cut] < 0
            lower = jnp.where(below, mixed[0], mixed[1])
            upper = jnp.where(below, mixed[1], mixed[2])
            part = lat_w[level, :, cut]
            field[step, level, :, cut] = (1.0 - part) * lower + part * upper

    def shift(chunk):
        levels = pl.ds(chunk * PER, PER)
        return pltpu.make_async_remote_copy(
            field.at[STEPS - 1, levels], prev.at[levels], shift_send.at[chunk], shift_recv.at[chunk],
            device_id={"win": win + 1}, device_id_type=MESH)

    for step in range(STEPS):
        for chunk in range(CHUNKS):
            @pl.when(has_south)
            def _():
                to_north(step, chunk).wait_recv()

            @pl.when(has_north)
            def _():
                to_south(step, chunk).wait_recv()

            @pl.when(has_next)
            def _():
                @pl.loop(chunk * PER, (chunk + 1) * PER)
                def _(level):
                    advance(step, level)

            if step < STEPS - 1:
                send_halo(step + 1, chunk)
            else:
                @pl.when(has_next)
                def _():
                    shift(chunk).start()

    for fetch in fetches[6:]:
        fetch.wait()

    my_rows = pl.ds(pl.multiple_of(lat * BAND, BAND), BAND)

    for chunk in range(CHUNKS):
        levels = pl.ds(chunk * PER, PER)

        @pl.when(has_prior)
        def _():
            shift(chunk).wait_recv()

        @pl.when(jnp.logical_not(has_prior))
        def _():
            prev[levels] = jnp.zeros((PER, BAND, NLON), jnp.float32)

        error = (pert[levels] - prev[levels]).reshape(PER * BAND, NLON)
        result = rows_times_table(error, fwd_high[...], fwd_low[...])
        for tile in range(TILES):
            coeffs[chunk, pl.ds(tile * PER, PER)] = result[:, tile * TILE : (tile + 1) * TILE].reshape(
                PER, BAND, TILE)

        @pl.loop(0, UNITS)
        def _(turn):
            side = jnp.where(turn < HALF_UNITS, 1 - half, half)
            place = (turn + column) % HALF_UNITS
            unit = side * HALF_UNITS + place
            target = owner_of(side, place, chunk)

            @pl.when(target != lat)
            def _():
                pltpu.make_async_remote_copy(
                    coeffs.at[chunk, unit], owned.at[chunk, my_rows], out_send.at[chunk], out_recv.at[chunk],
                    device_id={"lat": target}, device_id_type=MESH).start()

            @pl.when(target == lat)
            def _():
                pltpu.make_async_copy(
                    coeffs.at[chunk, unit], owned.at[chunk, my_rows], out_recv.at[chunk]).start()

    for share in range(5):
        piece = var_rows.at[pl.ds(share * SHARE, SHARE)]
        pltpu.make_async_copy(piece, piece, var_recv.at[share]).wait()
    pltpu.make_async_copy(rest_landing, rest_landing, var_recv.at[5]).wait()
    var_tile[...] = var_rows[...].T

    for chunk in range(CHUNKS):
        @pl.when(owns(chunk))
        def _():
            pltpu.make_async_copy(owned.at[chunk], owned.at[chunk], out_recv.at[chunk]).wait()
            modes = table_times_columns(basis_high[...], basis_low[...], owned[chunk])
            answer[chunk] = table_times_columns(
                basis_t_high[...], basis_t_low[...], modes * var_tile[...])

            @pl.loop(0, PEERS)
            def _(turn):
                peer = lat_of(jnp.where(turn < PEERS // 2, 1 - half, half), (turn + column) % (PEERS // 2))
                rows = pl.ds(pl.multiple_of(peer * BAND, BAND), BAND)

                @pl.when(peer != lat)
                def _():
                    pltpu.make_async_remote_copy(
                        answer.at[chunk, rows], returned.at[chunk, my_unit], back_send.at[chunk],
                        back_recv.at[chunk], device_id={"lat": peer}, device_id_type=MESH).start()

                @pl.when(peer == lat)
                def _():
                    pltpu.make_async_copy(
                        answer.at[chunk, rows], returned.at[chunk, my_unit], back_recv.at[chunk]).start()

    for chunk in range(CHUNKS):
        pltpu.make_async_copy(returned.at[chunk], returned.at[chunk], back_recv.at[chunk]).wait()
        rows = jnp.concatenate(
            [returned[chunk, pl.ds(tile * PER, PER)].reshape(PER * BAND, TILE) for tile in range(TILES)], axis=1)
        result = rows_times_table(rows, bwd_high[...], bwd_low[...])
        out[pl.ds(chunk * PER, PER)] = result.reshape(PER, BAND, NLON)

    for step in range(STEPS):
        for chunk in range(CHUNKS):
            @pl.when(has_north)
            def _():
                to_north(step, chunk).wait_send()

            @pl.when(has_south)
            def _():
                to_south(step, chunk).wait_send()

    for chunk in range(CHUNKS):
        @pl.when(has_next)
        def _():
            shift(chunk).wait_send()

        @pl.when(owns(chunk))
        def _():
            part = coeffs.at[chunk, pl.ds(0, UNITS - 1)]
            pltpu.make_async_copy(part, part, out_send.at[chunk]).wait()
            part = answer.at[chunk, pl.ds(0, NLAT - BAND)]
            pltpu.make_async_copy(part, part, back_send.at[chunk]).wait()

        @pl.when(jnp.logical_not(owns(chunk)))
        def _():
            part = coeffs.at[chunk]
            pltpu.make_async_copy(part, part, out_send.at[chunk]).wait()

    @pl.when(whole)
    def _():
        @pl.loop(0, share_count)
        def _(i):
            target = lat_of(half, share_first + i)

            @pl.when(target != lat)
            def _():
                share_to(target, i).wait_send()

    @pl.when(jnp.logical_not(whole))
    def _():
        @pl.loop(0, 15)
        def _(i):
            rest_to(lat_of(half, i), i).wait_send()


def body(perturbation, lat_offset, lon_offset, lat_weight, lon_weight, spectral_var):
    def levels_first(x):
        return jnp.transpose(x[0], (1, 0, 2))

    grid = (LEVELS, BAND, NLON)
    f32 = jnp.float32
    dma = pltpu.SemaphoreType.DMA
    operands = [
        *[levels_first(x) for x in (perturbation, lat_offset, lon_offset, lat_weight, lon_weight)],
        spectral_var.T,
        *[jnp.asarray(table) for table in tables()],
    ]
    result = pl.pallas_call(
        kernel,
        out_shape=jax.ShapeDtypeStruct(grid, f32),
        in_specs=[pl.BlockSpec(memory_space=pl.ANY)] * FETCHED,
        out_specs=pl.BlockSpec(memory_space=pltpu.VMEM),
        scratch_shapes=[
            *[pltpu.VMEM(x.shape, x.dtype) for x in operands],
            pltpu.VMEM((STEPS, *grid), f32),
            pltpu.VMEM((STEPS, *grid), f32),
            pltpu.VMEM((STEPS, *grid), f32),
            pltpu.VMEM(grid, f32),
            pltpu.VMEM((CHUNKS, UNITS, BAND, TILE), f32),
            pltpu.VMEM((CHUNKS, NLAT, TILE), f32),
            pltpu.VMEM((CHUNKS, NLAT, TILE), f32),
            pltpu.VMEM((CHUNKS, UNITS, BAND, TILE), f32),
            pltpu.VMEM((TILE, NLAT), f32),
            pltpu.VMEM((NLAT, TILE), f32),
            dma((2, STEPS, CHUNKS)),
            dma((2, STEPS, CHUNKS)),
            dma((CHUNKS,)),
            dma((CHUNKS,)),
            dma((CHUNKS,)),
            dma((CHUNKS,)),
            dma((CHUNKS,)),
            dma((CHUNKS,)),
            dma((15,)),
            dma((6,)),
            dma((FETCHED,)),
        ],
        compiler_params=pltpu.CompilerParams(
            collective_id=0, has_side_effects=True, vmem_limit_bytes=60 * 2**20),
    )(*operands)
    return jnp.transpose(result, (1, 0, 2))[None]


def solution(mesh):
    block = P("win", "lat", None, None)
    return jax.shard_map(
        body, mesh=mesh, in_specs=(block, block, block, block, block, P(None, "lat")), out_specs=block,
        check_vma=False)
```

```python
import math

import jax
import jax.numpy as jnp
import numpy as np
from jax import lax
from jax.experimental import pallas as pl
from jax.experimental.pallas import tpu as pltpu
from jax.sharding import PartitionSpec as P

STEPS = 4
MESH = pl.DeviceIdType.MESH

LEVELS, BAND, NLON, NLAT = 20, 8, 768, 256
CHUNKS = 5
PER = LEVELS // CHUNKS
TILE = 128
TILES = NLON // TILE
HALF_TILES = TILES // 2
UNITS = TILES * PER
HALF_UNITS = UNITS // 2
PEERS = NLAT // BAND
SHARE = NLON // PEERS
FETCHED = 14


def lat_of(half, column):
    inner = column < 8
    x = inner * (column // 2) + (1 - inner) * (column % 4)
    y = inner * (1 + column % 2) + (1 - inner) * (column // 12) * 3
    return (x * 2 + half) * 4 + y


def owner_of(half, place, chunk):
    return lat_of(half, place + 4 * (chunk % 2) * (place // 8))


def split_bf16(table):
    high = table.astype(jnp.bfloat16)
    low = (table - high.astype(np.float64)).astype(jnp.bfloat16)
    return high, low


def column_order():
    order = []
    for half in range(2):
        for tile in range(HALF_TILES):
            for column in range(5 * tile, 5 * tile + 5):
                order += [lat_of(half, column) * SHARE + i for i in range(SHARE)]
            order += [lat_of(half, 15) * SHARE + 8 * tile + i for i in range(8)]
    return np.array(order)


def tables():
    half_count = NLON // 2
    points = np.arange(NLON)[:, None]
    orders = np.arange(half_count)[None, :]
    angles = (points * orders % NLON) * (2.0 * math.pi / NLON)
    forward = np.concatenate([np.cos(angles), np.sin(angles)], axis=1)
    weights = np.where(orders == 0, 1.0, 2.0) / NLON
    backward = (forward * np.concatenate([weights, weights], axis=1)).T
    order = column_order()
    modes = np.arange(NLAT)[:, None]
    lats = np.arange(NLAT)[None, :]
    angles = ((2 * lats + 1) * modes % (4 * NLAT)) * (math.pi / (2 * NLAT))
    scaling = np.where(modes == 0, math.sqrt(1.0 / NLAT), math.sqrt(2.0 / NLAT))
    basis = scaling * np.cos(angles)
    return (
        *split_bf16(forward[:, order]),
        *split_bf16(backward[order, :]),
        *split_bf16(basis),
        *split_bf16(np.ascontiguousarray(basis.T)),
    )


def dot(a, b):
    return lax.dot_general(a, b, (((1,), (0,)), ((), ())), preferred_element_type=jnp.float32)


def rows_times_table(rows, high, low):
    count = rows.shape[0]
    rows_high = rows.astype(jnp.bfloat16).astype(jnp.float32)
    both = jnp.concatenate([rows_high, rows - rows_high], axis=0).astype(jnp.bfloat16)
    wide = dot(both, high)
    return wide[:count] + wide[count:] + dot(rows_high.astype(jnp.bfloat16), low)


def table_times_columns(high, low, columns):
    count = columns.shape[1]
    columns_high = columns.astype(jnp.bfloat16).astype(jnp.float32)
    both = jnp.concatenate([columns_high, columns - columns_high], axis=1).astype(jnp.bfloat16)
    wide = dot(high, both)
    return wide[:, :count] + wide[:, count:] + dot(low, columns_high.astype(jnp.bfloat16))


def kernel(
    *refs,
):
    sources, (out, *fetched), rest = refs[:FETCHED], refs[FETCHED : 2 * FETCHED + 1], refs[2 * FETCHED + 1 :]
    (pert, lat_off, lon_off, lat_w, lon_w, var,
     fwd_high, fwd_low, bwd_high, bwd_low, basis_high, basis_low, basis_t_high, basis_t_low) = fetched
    (
        field, from_south, from_north, prev, coeffs, owned, answer, returned, var_rows, var_tile,
        halo_send, halo_recv, shift_send, shift_recv, out_send, out_recv, back_send, back_recv, var_send, var_recv,
        fetch_sem,
    ) = rest
    fetches = [
        pltpu.make_async_copy(source, target, fetch_sem.at[i])
        for i, (source, target) in enumerate(zip(sources, fetched))
    ]
    fetches[0].start()

    win = lax.axis_index("win")
    lat = lax.axis_index("lat")
    windows = lax.axis_size("win")
    half = (lat // 4) % 2
    x, y = lat // 8, lat % 4
    column = jnp.where(y == 0, 8 + x, jnp.where(y == 3, 12 + x, 2 * x + y - 1))
    inner = column < 8
    my_unit = half * HALF_UNITS + jnp.where(inner, column, 8 + x)

    def owns(chunk):
        return inner | (y == 0 if chunk % 2 == 0 else y == 3)

    has_prior = win > 0
    has_next = win < windows - 1
    has_south = has_next & (lat > 0)
    has_north = has_next & (lat < PEERS - 1)

    barrier = pltpu.get_barrier_semaphore()

    @pl.loop(0, PEERS)
    def _(turn):
        peer = lat_of(jnp.where(turn < PEERS // 2, 1 - half, half), turn % (PEERS // 2))

        @pl.when(peer != lat)
        def _():
            pl.semaphore_signal(barrier, 1, device_id={"lat": peer}, device_id_type=MESH)

    @pl.when(has_prior)
    def _():
        pl.semaphore_signal(barrier, 1, device_id={"win": win - 1}, device_id_type=MESH)

    @pl.when(has_next)
    def _():
        pl.semaphore_signal(barrier, 1, device_id={"win": win + 1}, device_id_type=MESH)

    for fetch in fetches[1:]:
        fetch.start()

    @pl.when(jnp.logical_not(has_south))
    def _():
        from_south[...] = jnp.zeros_like(from_south)

    @pl.when(jnp.logical_not(has_north))
    def _():
        from_north[...] = jnp.zeros_like(from_north)

    fetches[0].wait()
    pl.semaphore_wait(barrier, PEERS - 1 + has_prior.astype(jnp.int32) + has_next.astype(jnp.int32))

    def source(step):
        return pert if step == 0 else field.at[step - 1]

    def to_north(step, chunk):
        levels = pl.ds(chunk * PER, PER)
        return pltpu.make_async_remote_copy(
            source(step).at[levels, pl.ds(BAND - 1, 1)], from_south.at[step, levels, pl.ds(BAND - 1, 1)],
            halo_send.at[0, step, chunk], halo_recv.at[0, step, chunk],
            device_id={"lat": lat + 1}, device_id_type=MESH)

    def to_south(step, chunk):
        levels = pl.ds(chunk * PER, PER)
        return pltpu.make_async_remote_copy(
            source(step).at[levels, pl.ds(0, 1)], from_north.at[step, levels, pl.ds(0, 1)],
            halo_send.at[1, step, chunk], halo_recv.at[1, step, chunk],
            device_id={"lat": lat - 1}, device_id_type=MESH)

    def send_halo(step, chunk):
        @pl.when(has_north)
        def _():
            to_north(step, chunk).start()

        @pl.when(has_south)
        def _():
            to_south(step, chunk).start()

    for chunk in range(CHUNKS):
        send_halo(0, chunk)

    for fetch in fetches[1:6]:
        fetch.wait()

    whole = column < 15
    share_tile = column // 5
    share_first = share_tile * PER
    share_count = jnp.where(share_tile == 2, 2 * PER, PER)
    landing = var_rows.at[pl.ds(pl.multiple_of((column % 5) * SHARE, 8), SHARE)]
    rest_landing = var_rows.at[pl.ds(5 * SHARE, 8)]

    def share_to(target, i):
        return pltpu.make_async_remote_copy(
            var, landing, var_send.at[i], var_recv.at[column % 5], device_id={"lat": target}, device_id_type=MESH)

    def rest_to(target, i):
        tile = jnp.minimum(i // PER, 2)
        return pltpu.make_async_remote_copy(
            var.at[pl.ds(pl.multiple_of(8 * tile, 8), 8)], rest_landing, var_send.at[i], var_recv.at[5],
            device_id={"lat": target}, device_id_type=MESH)

    @pl.when(whole)
    def _():
        @pl.loop(0, share_count)
        def _(i):
            target = lat_of(half, share_first + i)

            @pl.when(target != lat)
            def _():
                share_to(target, i).start()

            @pl.when(target == lat)
            def _():
                pltpu.make_async_copy(var, landing, var_recv.at[column % 5]).start()

    @pl.when(jnp.logical_not(whole))
    def _():
        @pl.loop(0, 15)
        def _(i):
            rest_to(lat_of(half, i), i).start()

        pltpu.make_async_copy(var.at[pl.ds(16, 8)], rest_landing, var_recv.at[5]).start()

    rows_at = lax.broadcasted_iota(jnp.int32, (BAND, NLON), 0)
    lane = lax.broadcasted_iota(jnp.int32, (BAND, TILE), 1)

    def advance(step, level):
        here = source(step)[level]
        south = pltpu.roll(
            jnp.where(rows_at == BAND - 1, from_south[step, level, pl.ds(BAND - 1, 1)], here), 1, 0)
        north = pltpu.roll(
            jnp.where(rows_at == 0, from_north[step, level, pl.ds(0, 1)], here), BAND - 1, 0)
        for tile in range(TILES):
            cut = slice(tile * TILE, (tile + 1) * TILE)
            west = lane + lon_off[level, :, cut]
            east = west + 1
            west_in = (west >= 0) & (west < TILE)
            east_in = (east >= 0) & (east < TILE)
            west = west & (TILE - 1)
            east = east & (TILE - 1)
            weight = lon_w[level, :, cut]
            mixed = []
            for rows in (south, here, north):
                middle = rows[:, cut]
                after = (tile + 1) % TILES * TILE
                before = (tile - 1) % TILES * TILE
                beside = jnp.where(
                    lane < TILE // 2, rows[:, after : after + TILE], rows[:, before : before + TILE])
                near = jnp.where(
                    west_in, jnp.take_along_axis(middle, west, 1), jnp.take_along_axis(beside, west, 1))
                far = jnp.where(
                    east_in, jnp.take_along_axis(middle, east, 1), jnp.take_along_axis(beside, east, 1))
                mixed.append((1.0 - weight) * near + weight * far)
            below = lat_off[level, :, cut] < 0
            lower = jnp.where(below, mixed[0], mixed[1])
            upper = jnp.where(below, mixed[1], mixed[2])
            part = lat_w[level, :, cut]
            field[step, level, :, cut] = (1.0 - part) * lower + part * upper

    def shift(chunk):
        levels = pl.ds(chunk * PER, PER)
        return pltpu.make_async_remote_copy(
            field.at[STEPS - 1, levels], prev.at[levels], shift_send.at[chunk], shift_recv.at[chunk],
            device_id={"win": win + 1}, device_id_type=MESH)

    for step in range(STEPS):
        for chunk in range(CHUNKS):
            @pl.when(has_south)
            def _():
                to_north(step, chunk).wait_recv()

            @pl.when(has_north)
            def _():
                to_south(step, chunk).wait_recv()

            @pl.when(has_next)
            def _():
                @pl.loop(chunk * PER, (chunk + 1) * PER)
                def _(level):
                    advance(step, level)

            if step < STEPS - 1:
                send_halo(step + 1, chunk)
            else:
                @pl.when(has_next)
                def _():
                    shift(chunk).start()

    for fetch in fetches[6:]:
        fetch.wait()

    my_rows = pl.ds(pl.multiple_of(lat * BAND, BAND), BAND)

    for chunk in range(CHUNKS):
        levels = pl.ds(chunk * PER, PER)

        @pl.when(has_prior)
        def _():
            shift(chunk).wait_recv()

        @pl.when(jnp.logical_not(has_prior))
        def _():
            prev[levels] = jnp.zeros((PER, BAND, NLON), jnp.float32)

        error = (pert[levels] - prev[levels]).reshape(PER * BAND, NLON)
        result = rows_times_table(error, fwd_high[...], fwd_low[...])
        for tile in range(TILES):
            coeffs[chunk, pl.ds(tile * PER, PER)] = result[:, tile * TILE : (tile + 1) * TILE].reshape(
                PER, BAND, TILE)

        @pl.loop(0, UNITS)
        def _(turn):
            side = jnp.where(turn < HALF_UNITS, 1 - half, half)
            place = (turn + column) % HALF_UNITS
            unit = side * HALF_UNITS + place
            target = owner_of(side, place, chunk)

            @pl.when(target != lat)
            def _():
                pltpu.make_async_remote_copy(
                    coeffs.at[chunk, unit], owned.at[chunk, my_rows], out_send.at[chunk], out_recv.at[chunk],
                    device_id={"lat": target}, device_id_type=MESH).start()

            @pl.when(target == lat)
            def _():
                pltpu.make_async_copy(
                    coeffs.at[chunk, unit], owned.at[chunk, my_rows], out_recv.at[chunk]).start()

    for share in range(5):
        piece = var_rows.at[pl.ds(share * SHARE, SHARE)]
        pltpu.make_async_copy(piece, piece, var_recv.at[share]).wait()
    pltpu.make_async_copy(rest_landing, rest_landing, var_recv.at[5]).wait()
    var_tile[...] = var_rows[...].T

    for chunk in range(CHUNKS):
        @pl.when(owns(chunk))
        def _():
            pltpu.make_async_copy(owned.at[chunk], owned.at[chunk], out_recv.at[chunk]).wait()
            modes = table_times_columns(basis_high[...], basis_low[...], owned[chunk])
            answer[chunk] = table_times_columns(
                basis_t_high[...], basis_t_low[...], modes * var_tile[...])

            @pl.loop(0, PEERS)
            def _(turn):
                peer = lat_of(jnp.where(turn < PEERS // 2, 1 - half, half), (turn + column) % (PEERS // 2))
                rows = pl.ds(pl.multiple_of(peer * BAND, BAND), BAND)

                @pl.when(peer != lat)
                def _():
                    pltpu.make_async_remote_copy(
                        answer.at[chunk, rows], returned.at[chunk, my_unit], back_send.at[chunk],
                        back_recv.at[chunk], device_id={"lat": peer}, device_id_type=MESH).start()

                @pl.when(peer == lat)
                def _():
                    pltpu.make_async_copy(
                        answer.at[chunk, rows], returned.at[chunk, my_unit], back_recv.at[chunk]).start()

    for chunk in range(CHUNKS):
        pltpu.make_async_copy(returned.at[chunk], returned.at[chunk], back_recv.at[chunk]).wait()
        rows = jnp.concatenate(
            [returned[chunk, pl.ds(tile * PER, PER)].reshape(PER * BAND, TILE) for tile in range(TILES)], axis=1)
        result = rows_times_table(rows, bwd_high[...], bwd_low[...])
        out[pl.ds(chunk * PER, PER)] = result.reshape(PER, BAND, NLON)

    for step in range(STEPS):
        for chunk in range(CHUNKS):
            @pl.when(has_north)
            def _():
                to_north(step, chunk).wait_send()

            @pl.when(has_south)
            def _():
                to_south(step, chunk).wait_send()

    for chunk in range(CHUNKS):
        @pl.when(has_next)
        def _():
            shift(chunk).wait_send()

        @pl.when(owns(chunk))
        def _():
            part = coeffs.at[chunk, pl.ds(0, UNITS - 1)]
            pltpu.make_async_copy(part, part, out_send.at[chunk]).wait()
            part = answer.at[chunk, pl.ds(0, NLAT - BAND)]
            pltpu.make_async_copy(part, part, back_send.at[chunk]).wait()

        @pl.when(jnp.logical_not(owns(chunk)))
        def _():
            part = coeffs.at[chunk]
            pltpu.make_async_copy(part, part, out_send.at[chunk]).wait()

    @pl.when(whole)
    def _():
        @pl.loop(0, share_count)
        def _(i):
            target = lat_of(half, share_first + i)

            @pl.when(target != lat)
            def _():
                share_to(target, i).wait_send()

    @pl.when(jnp.logical_not(whole))
    def _():
        @pl.loop(0, 15)
        def _(i):
            rest_to(lat_of(half, i), i).wait_send()


def body(perturbation, lat_offset, lon_offset, lat_weight, lon_weight, spectral_var):
    def levels_first(x):
        return jnp.transpose(x[0], (1, 0, 2))

    grid = (LEVELS, BAND, NLON)
    f32 = jnp.float32
    dma = pltpu.SemaphoreType.DMA
    operands = [
        *[levels_first(x) for x in (perturbation, lat_offset, lon_offset, lat_weight, lon_weight)],
        spectral_var.T,
        *[jnp.asarray(table) for table in tables()],
    ]
    result = pl.pallas_call(
        kernel,
        out_shape=jax.ShapeDtypeStruct(grid, f32),
        in_specs=[pl.BlockSpec(memory_space=pl.ANY)] * FETCHED,
        out_specs=pl.BlockSpec(memory_space=pltpu.VMEM),
        scratch_shapes=[
            *[pltpu.VMEM(x.shape, x.dtype) for x in operands],
            pltpu.VMEM((STEPS, *grid), f32),
            pltpu.VMEM((STEPS, *grid), f32),
            pltpu.VMEM((STEPS, *grid), f32),
            pltpu.VMEM(grid, f32),
            pltpu.VMEM((CHUNKS, UNITS, BAND, TILE), f32),
            pltpu.VMEM((CHUNKS, NLAT, TILE), f32),
            pltpu.VMEM((CHUNKS, NLAT, TILE), f32),
            pltpu.VMEM((CHUNKS, UNITS, BAND, TILE), f32),
            pltpu.VMEM((TILE, NLAT), f32),
            pltpu.VMEM((NLAT, TILE), f32),
            dma((2, STEPS, CHUNKS)),
            dma((2, STEPS, CHUNKS)),
            dma((CHUNKS,)),
            dma((CHUNKS,)),
            dma((CHUNKS,)),
            dma((CHUNKS,)),
            dma((CHUNKS,)),
            dma((CHUNKS,)),
            dma((15,)),
            dma((6,)),
            dma((FETCHED,)),
        ],
        compiler_params=pltpu.CompilerParams(
            collective_id=0, has_side_effects=True, vmem_limit_bytes=60 * 2**20),
    )(*operands)
    return jnp.transpose(result, (1, 0, 2))[None]


def solution(mesh):
    block = P("win", "lat", None, None)
    return jax.shard_map(
        body, mesh=mesh, in_specs=(block, block, block, block, block, P(None, "lat")), out_specs=block,
        check_vma=False)
```
